512 devices in a mesh: row: 32 (over y, x), col: 16 (over z, core).
Axes of the slice: x: 4, y: 8, z: 8, core: 2. Of those that a mesh axis runs over, the one named last changes fastest.
Arguments:
- matrix: float32 [12288, 12288], P('row', 'col'), may hold values from 0 to 2, as said below
Outputs:
- factored: float32 [12288, 12288], P('row', 'col')
The draws below stay inside these ranges and needn't reach their ends.
Inputs may be any that keep to these rules, and one draw needn't show every extreme that they name: `matrix`: symmetric positive definite: a Matern kernel of smoothness 3/2 over points, plus a positive noise term on the diagonal.
All inputs are finite; a program needn't handle non-finite values.
Results may differ from the reference program's by a relative error of at most 0.0003.
Values sent between devices are 32-bit elements; how exact they have to be, the bound alone decides.
No kernel may reach another device: no remote copies, remote signals or barrier semaphores. Data moves between devices by JAX's collectives and lax.ppermute only.
A program may use at most 64 MiB of HBM per device.

```python
import jax
import jax.numpy as jnp
from jax import lax

M = 12288
NB = 512
PANELS = 2
BS = 32
N_ROW = 32
N_COL = 16


LENGTH_SCALE = 2.0


def stored_order(logical):
    by_rows = logical.reshape(M // (N_ROW * BS), N_ROW, BS, M).transpose(1, 0, 2, 3).reshape(M, M)
    return by_rows.reshape(M, M // (N_COL * BS), N_COL, BS).transpose(0, 2, 1, 3).reshape(M, M)


def draw_matrix(key, part):
    key = jax.random.fold_in(key, 7)
    key_points, key_jitter = jax.random.split(key, 2)
    points = jax.random.normal(key_points, (M, 8), jnp.float32)
    jitter_diag = jnp.exp(jax.random.uniform(key_jitter, (M,), jnp.float32, jnp.log(0.1), 0.0))
    squares = jnp.sum(points * points, axis=1)
    distance_sq = squares[:, None] + squares[None, :] - 2.0 * jnp.dot(points, points.T)
    distance_sq = jnp.maximum(distance_sq, 0.0)
    scaled = jnp.sqrt(3.0) * jnp.sqrt(distance_sq) / LENGTH_SCALE
    kernel = (1.0 + scaled) * jnp.exp(-scaled)
    kernel = 0.5 * (kernel + kernel.T)
    kernel = kernel + jnp.diag(jitter_diag)
    return stored_order(kernel).astype(jnp.float32)


def setup_inputs(seed: int = 0) -> dict:
    arg_keys = jax.random.split(jax.random.key(seed), 2)
    return {
        "matrix": draw_matrix(jax.random.fold_in(arg_keys[1], 71), 0),
    }


def to_logical(stored):
    by_rows = stored.reshape(N_ROW, M // (N_ROW * BS), BS, M).transpose(1, 0, 2, 3).reshape(M, M)
    return by_rows.reshape(M, N_COL, M // (N_COL * BS), BS).transpose(0, 2, 1, 3).reshape(M, M)

def to_stored(logical):
    by_rows = logical.reshape(M // (N_ROW * BS), N_ROW, BS, M).transpose(1, 0, 2, 3).reshape(M, M)
    return by_rows.reshape(M, M // (N_COL * BS), N_COL, BS).transpose(0, 2, 1, 3).reshape(M, M)

def reference(matrix):
    logical = to_logical(matrix)
    for panel_index in range(PANELS):
        start_col = panel_index * NB
        end_col = start_col + NB
        factor = jnp.linalg.cholesky(logical[start_col:end_col, start_col:end_col])
        panel_rows = jax.scipy.linalg.solve_triangular(factor, logical[start_col:, start_col:end_col].T, lower=True).T
        trailing = panel_rows[NB:]
        update = jnp.dot(trailing, trailing.T, precision=lax.Precision.HIGHEST)
        logical = logical.at[end_col:, end_col:].add(-update)
        full_panel = jnp.concatenate([jnp.zeros((start_col, NB), jnp.float32), panel_rows], axis=0)
        logical = logical.at[:, start_col:end_col].set(full_panel)
    return to_stored(logical)
```

```python
import jax
import jax.numpy as jnp
from jax import lax
from jax.experimental import pallas as pl
from jax.experimental.pallas import tpu as pltpu
from jax.sharding import Mesh
from jax.sharding import PartitionSpec as P

NB = 512
PANELS = 2
BS = 32
PR = NB * PANELS
B = 128
KB = PR // B

f32 = jnp.float32
bf16 = jnp.bfloat16
NN = (((1,), (0,)), ((), ()))
NT = (((1,), (1,)), ((), ()))


def split(x):
    hi = x.astype(bf16)
    lo = (x - hi.astype(f32)).astype(bf16)
    return hi, lo


def dot(a, b, dims):
    return lax.dot_general(a, b, dims, preferred_element_type=f32)


def dot3(a, b, dims):
    ah, al = a
    bh, bl = b
    return dot(ah, bh, dims) + (dot(ah, bl, dims) + dot(al, bh, dims))


def tree(terms):
    while len(terms) > 1:
        terms = [sum(terms[i : i + 2][1:], terms[i]) for i in range(0, len(terms), 2)]
    return terms[0]


def lane_b(x, lane):
    return jnp.broadcast_to(x[:, lane : lane + 1], (8, 128))


def sub_b(x, row):
    return jnp.broadcast_to(x[row : row + 1, :], (8, 128))


def factor128(d_ref, y_ref, g_ref, lbt_ref, fill):
    row = lax.broadcasted_iota(jnp.int32, (8, 128), 0)
    lane = lax.broadcasted_iota(jnp.int32, (8, 128), 1)
    S = [d_ref[8 * s : 8 * s + 8, :] for s in range(16)]
    G = [jnp.where(lane == row + 8 * s, 1.0, 0.0).astype(f32) for s in range(16)]

    def column(vals):
        v = vals[7]
        for t in range(6, -1, -1):
            v = jnp.where(row == t, vals[t], v)
        return v

    for s in range(16):
        c = [lane_b(S[s], 8 * s + m) for m in range(8)]
        a = {(t, m): sub_b(c[m], t) for m in range(8) for t in range(m, 8)}
        M = {}
        d = []
        for i in range(8):
            pivot = a[i, i]
            p = 1.0 / pivot
            d.append(pivot)
            old = {j: a[max(i, j), min(i, j)] for j in range(8) if j != i}
            scaled = {j: old[j] * p for j in old}
            for j in old:
                if j > i:
                    M[j, i] = scaled[j]
            for k in old:
                for j in old:
                    if j <= k:
                        a[k, j] = a[k, j] - old[j] * scaled[k]
            for j in old:
                a[max(i, j), min(i, j)] = scaled[j]
            a[i, i] = -p
        w = [column([a[max(t, m), min(t, m)] for t in range(8)]) for m in range(8)]
        YS = tree([w[m] * sub_b(S[s], m) for m in range(8)])
        YG = tree([w[m] * sub_b(G[s], m) for m in range(8)])
        y_ref[8 * s : 8 * s + 8, :] = -YG
        g_ref[8 * s : 8 * s + 8, :] = G[s]
        ys = [sub_b(YS, m) for m in range(8)]
        yg = [sub_b(YG, m) for m in range(8)]
        for r in range(s + 1, 16):
            b = [lane_b(S[r], 8 * s + m) for m in range(8)]
            S[r] = S[r] + tree([b[m] * ys[m] for m in range(8)])
            G[r] = G[r] + tree([b[m] * yg[m] for m in range(8)])
        sq = [jnp.sqrt(d[i]) for i in range(8)]
        zero = jnp.zeros((8, 128), f32)
        lb = zero
        for t in range(8):
            vals = [M[t, i] * sq[i] for i in range(t)] + [sq[t]] + [zero] * (7 - t)
            lb = jnp.where(lane == 8 * s + t, column(vals), lb)
        lbt_ref[8 * s : 8 * s + 8, :] = lb
        fill(s)


def factor_and_update(ids, gathered, a_cols, local):
    RR, CC = local.shape
    W = PR + RR + CC
    n_col = PR // (PANELS * BS)

    def kern(id_ref, pr_ref, ac, al, out, E, D, Y, G, LBT, YQ, GQ, LQ, LT, RHH, RLO, LRH, LRL, ZCH, ZCL, XT):
        for c in range(n_col):
            for p in range(PANELS):
                src = (c * PANELS + p) * BS
                dst = p * NB + c * BS
                E[dst : dst + BS, 0 : PR + RR] = pr_ref[src : src + BS, :]
        E[:, PR + RR :] = ac[...]
        D[...] = E[0:B, 0:B]
        for ref in (YQ, GQ, LQ):
            ref[...] = jnp.zeros(ref.shape, bf16)
        rid = id_ref[0]
        cid = id_ref[1]
        second = rid >= NB // BS
        lane_r = lax.broadcasted_iota(jnp.int32, (B, RR), 1)

        def panel_chunks(q, q0, with_p):
            def eq(c0, w):
                return split(E[pl.ds(q0, B), c0 : c0 + w])

            def yq():
                return YQ[0], YQ[1]

            def gq():
                return GQ[0], GQ[1]

            def keep(c0, w, h, l):
                RHH[0:B, c0 : c0 + w] = h
                RHH[B : 2 * B, c0 : c0 + w] = h
                RLO[:, c0 : c0 + w] = l

            def row_panel(c0, w):
                def f():
                    h, l = split(dot3(yq(), eq(c0, w), NN))
                    keep(c0, w, h, l)
                    if c0 >= PR + RR:
                        cc = c0 - PR - RR
                        ZCH[pl.ds(q0, B), cc : cc + w] = h
                        ZCL[pl.ds(q0, B), cc : cc + w] = l

                return f

            def r_panel():
                e = eq(PR, RR)
                zp = split(dot3(yq(), e, NN))
                keep(PR, RR, *zp)
                XT[pl.ds(q0, B), :] = dot3((LQ[0], LQ[1]), zp, NN)
                zr = dot3(gq(), e, NN)
                live = jnp.logical_and(second, q < NB // B)
                zr = jnp.where(jnp.logical_and(lane_r < BS, jnp.logical_not(live)), 0.0, zr)
                h, l = split(zr.T)
                LRH[:, pl.ds(q0, B)] = h
                LRL[:, pl.ds(q0, B)] = l

            def col_panel(j):
                def f():
                    e = split(E[j * B : (j + 1) * B, pl.ds(q0, B)])
                    h, l = split(dot3(e, gq(), NT))
                    LT[j * B : (j + 1) * B, 0:B] = h
                    LT[j * B : (j + 1) * B, B : 2 * B] = l

                return f

            chunks = []
            if with_p:
                chunks += [col_panel(j) for j in range(KB)]
                chunks += [row_panel(c0, 256) for c0 in range(0, PR, 256)]
            chunks += [row_panel(c0, 256) for c0 in range(PR + RR, W, 256)]
            return chunks + [r_panel]

        def trail_chunks():
            def trail(j, c0, w):
                def f():
                    rows = slice(j * B, (j + 1) * B)
                    u = dot(LT[rows, :], RHH[:, c0 : c0 + w], NN)
                    u = u + dot(LT[rows, 0:B], RLO[:, c0 : c0 + w], NN)
                    E[rows, c0 : c0 + w] = E[rows, c0 : c0 + w] - u

                return f

            parts = ((0, 512), (512, 512), (PR, RR), (PR + RR, CC))
            return [trail(j, c0, w) for j in range(KB) for c0, w in parts]

        def body(k, carry):
            q = jnp.maximum(k - 1, 0)
            q0 = pl.multiple_of(q * B, B)
            k0 = pl.multiple_of(k * B, B)
            n0 = pl.multiple_of(jnp.minimum(k + 1, KB - 1) * B, B)
            chunks = panel_chunks(q, q0, True) + trail_chunks()
            n = len(chunks)

            def fill(s):
                for f in chunks[n * s // 16 : n * (s + 1) // 16]:
                    f()

            factor128(D, Y, G, LBT, fill)
            y = split(Y[...])
            g = split(G[...])
            lb = split(LBT[...])
            for i in range(2):
                YQ[i] = y[i]
                GQ[i] = g[i]
                LQ[i] = lb[i]
            zp = split(dot3(y, split(E[pl.ds(k0, B), pl.ds(n0, B)]), NN))
            zt = split(dot3(split(E[pl.ds(n0, B), pl.ds(k0, B)]), g, NT))
            D[...] = E[pl.ds(n0, B), pl.ds(n0, B)] - dot3(zt, zp, NN)
            return carry

        lax.fori_loop(0, KB, body, 0)
        for f in panel_chunks(KB - 1, (KB - 1) * B, False):
            f()
        for c0 in range(0, CC, 256):
            zh = ZCH[:, c0 : c0 + 256]
            zl = ZCL[:, c0 : c0 + 256]
            u = dot(LRH[...], zh, NN) + (dot(LRH[...], zl, NN) + dot(LRL[...], zh, NN))
            out[:, c0 : c0 + 256] = al[:, c0 : c0 + 256] - u
        for p in range(PANELS):
            c0 = pl.multiple_of(cid * BS + p * NB, BS)
            x = XT[pl.ds(c0, BS), :]
            col = c0 + lax.broadcasted_iota(jnp.int32, (BS, RR), 0)
            ln = lax.broadcasted_iota(jnp.int32, (BS, RR), 1)
            x = jnp.where(jnp.logical_and(ln < BS, col > rid * BS + ln), 0.0, x)
            out[:, BS * p : BS * (p + 1)] = x.T

    vm = pl.BlockSpec(memory_space=pltpu.VMEM)
    V = pltpu.VMEM
    return pl.pallas_call(
        kern,
        out_shape=jax.ShapeDtypeStruct((RR, CC), f32),
        in_specs=[pl.BlockSpec(memory_space=pltpu.SMEM)] + [vm] * 3,
        out_specs=vm,
        scratch_shapes=[
            V((PR, W), f32),
            V((B, B), f32),
            V((B, B), f32),
            V((B, B), f32),
            V((B, B), f32),
            V((2, B, B), bf16),
            V((2, B, B), bf16),
            V((2, B, B), bf16),
            V((PR, 2 * B), bf16),
            V((2 * B, W), bf16),
            V((B, W), bf16),
            V((RR, PR), bf16),
            V((RR, PR), bf16),
            V((PR, CC), bf16),
            V((PR, CC), bf16),
            V((PR, RR), f32),
        ],
        compiler_params=pltpu.CompilerParams(vmem_limit_bytes=40 * 1024 * 1024),
        name="factor_and_update",
    )(ids, gathered, a_cols, local)


def shards(matrix):
    rid = lax.axis_index(("y", "x"))
    cid = lax.axis_index(("z", "k"))
    ids = jnp.stack([rid, cid]).astype(jnp.int32)
    n_row = lax.axis_size(("y", "x"))
    thin = PANELS * BS
    a_cols = lax.all_gather(matrix[:BS], "x", axis=0, tiled=True)
    a_cols = lax.all_gather(a_cols, "y", axis=0, tiled=True)
    block = matrix[:BS, :thin].reshape(1, BS * thin // 128, 128)
    block = jnp.broadcast_to(block, (n_row, BS * thin // 128, 128))
    own = lax.all_to_all(block, ("y", "x"), 0, 0, tiled=True).reshape(PR, thin).T
    mine = jnp.concatenate([own, matrix[:, :thin].T], axis=1)
    gathered = lax.all_gather(mine, ("z", "k"), axis=0, tiled=True)
    return factor_and_update(ids, gathered, a_cols, matrix)


def solution(mesh):
    four = Mesh(mesh.devices.reshape(8, 4, 8, 2), ("y", "x", "z", "k"))
    placed = P(("y", "x"), ("z", "k"))
    return jax.shard_map(shards, mesh=four, in_specs=(placed,), out_specs=placed, check_vma=False)
```

```python
import jax
import jax.numpy as jnp
from jax import lax
from jax.experimental import pallas as pl
from jax.experimental.pallas import tpu as pltpu
from jax.sharding import Mesh
from jax.sharding import PartitionSpec as P

NB = 512
PANELS = 2
BS = 32
PR = NB * PANELS
B = 128
KB = PR // B

f32 = jnp.float32
bf16 = jnp.bfloat16
NN = (((1,), (0,)), ((), ()))
NT = (((1,), (1,)), ((), ()))


def split(x):
    hi = x.astype(bf16)
    lo = (x - hi.astype(f32)).astype(bf16)
    return hi, lo


def dot(a, b, dims):
    return lax.dot_general(a, b, dims, preferred_element_type=f32)


def dot3(a, b, dims):
    ah, al = a
    bh, bl = b
    return dot(ah, bh, dims) + (dot(ah, bl, dims) + dot(al, bh, dims))


def tree(terms):
    while len(terms) > 1:
        terms = [sum(terms[i : i + 2][1:], terms[i]) for i in range(0, len(terms), 2)]
    return terms[0]


def lane_b(x, lane):
    return jnp.broadcast_to(x[:, lane : lane + 1], (8, 128))


def sub_b(x, row):
    return jnp.broadcast_to(x[row : row + 1, :], (8, 128))


def factor128(d_ref, y_ref, g_ref, lbt_ref, fill):
    row = lax.broadcasted_iota(jnp.int32, (8, 128), 0)
    lane = lax.broadcasted_iota(jnp.int32, (8, 128), 1)
    S = [d_ref[8 * s : 8 * s + 8, :] for s in range(16)]
    G = [jnp.where(lane == row + 8 * s, 1.0, 0.0).astype(f32) for s in range(16)]

    def column(vals):
        v = vals[7]
        for t in range(6, -1, -1):
            v = jnp.where(row == t, vals[t], v)
        return v

    for s in range(16):
        c = [lane_b(S[s], 8 * s + m) for m in range(8)]
        a = {(t, m): sub_b(c[m], t) for m in range(8) for t in range(m, 8)}
        M = {}
        d = []
        for i in range(8):
            pivot = a[i, i]
            p = 1.0 / pivot
            d.append(pivot)
            old = {j: a[max(i, j), min(i, j)] for j in range(8) if j != i}
            scaled = {j: old[j] * p for j in old}
            for j in old:
                if j > i:
                    M[j, i] = scaled[j]
            for k in old:
                for j in old:
                    if j <= k:
                        a[k, j] = a[k, j] - old[j] * scaled[k]
            for j in old:
                a[max(i, j), min(i, j)] = scaled[j]
            a[i, i] = -p
        w = [column([a[max(t, m), min(t, m)] for t in range(8)]) for m in range(8)]
        YS = tree([w[m] * sub_b(S[s], m) for m in range(8)])
        YG = tree([w[m] * sub_b(G[s], m) for m in range(8)])
        y_ref[8 * s : 8 * s + 8, :] = -YG
        g_ref[8 * s : 8 * s + 8, :] = G[s]
        ys = [sub_b(YS, m) for m in range(8)]
        yg = [sub_b(YG, m) for m in range(8)]
        for r in range(s + 1, 16):
            b = [lane_b(S[r], 8 * s + m) for m in range(8)]
            S[r] = S[r] + tree([b[m] * ys[m] for m in range(8)])
            G[r] = G[r] + tree([b[m] * yg[m] for m in range(8)])
        sq = [jnp.sqrt(d[i]) for i in range(8)]
        zero = jnp.zeros((8, 128), f32)
        lb = zero
        for t in range(8):
            vals = [M[t, i] * sq[i] for i in range(t)] + [sq[t]] + [zero] * (7 - t)
            lb = jnp.where(lane == 8 * s + t, column(vals), lb)
        lbt_ref[8 * s : 8 * s + 8, :] = lb
        fill(s)


def drain(chunks):
    for f in chunks:
        f()


def crit(E, D, Y, G, k0, n0):
    zp = split(dot3(Y, split(E[pl.ds(k0, B), pl.ds(n0, B)]), NN))
    zt = split(dot3(split(E[pl.ds(n0, B), pl.ds(k0, B)]), G, NT))
    D[...] = E[pl.ds(n0, B), pl.ds(n0, B)] - dot3(zt, zp, NN)


def panel_solve(ids, gathered):
    W = gathered.shape[1]
    RR = W - PR
    n_col = PR // (PANELS * BS)

    def kern(id_ref, pr_ref, vth, vtl, xc, E, D, Y, G, LBT, YQ, GQ, LQ, LT, RHH, RLO, ZPH, ZPL, ZR, GTH, GTL, VH, VL, XT, sems):
        copies = []
        for c in range(n_col):
            for p in range(PANELS):
                n = c * PANELS + p
                copies.append(
                    pltpu.make_async_copy(
                        pr_ref.at[pl.ds(n * BS, BS), :], E.at[pl.ds(p * NB + c * BS, BS), :], sems.at[n]
                    )
                )
        for copy in copies:
            copy.start()
        for ref in (YQ, GQ, LQ):
            ref[...] = jnp.zeros(ref.shape, bf16)
        for copy in copies:
            copy.wait()
        D[...] = E[0:B, 0:B]
        rid = id_ref[0]
        cid = id_ref[1]
        second = rid >= NB // BS
        lane_r = lax.broadcasted_iota(jnp.int32, (B, RR), 1)

        def panel_chunks(q, q0, with_p):
            def yq():
                return YQ[0], YQ[1]

            def gq():
                return GQ[0], GQ[1]

            def keep(c0, w, h, l):
                RHH[0:B, c0 : c0 + w] = h
                RHH[B : 2 * B, c0 : c0 + w] = h
                RLO[:, c0 : c0 + w] = l

            def row_panel(c0, w):
                def f():
                    h, l = split(dot3(yq(), split(E[pl.ds(q0, B), c0 : c0 + w]), NN))
                    keep(c0, w, h, l)
                    ZPH[pl.ds(q0, B), c0 : c0 + w] = h
                    ZPL[pl.ds(q0, B), c0 : c0 + w] = l

                return f

            def r_panel():
                z = dot3(yq(), split(E[pl.ds(q0, B), PR:W]), NN)
                zp = split(z)
                keep(PR, RR, *zp)
                XT[pl.ds(q0, B), :] = dot3((LQ[0], LQ[1]), zp, NN)
                live = jnp.logical_and(second, q < NB // B)
                ZR[pl.ds(q0, B), :] = jnp.where(jnp.logical_and(lane_r < BS, jnp.logical_not(live)), 0.0, z)

            def transposed():
                h, l = split((gq()[0].astype(f32) + gq()[1].astype(f32)).T)
                GTH[pl.ds(q0, B), :] = h
                GTL[pl.ds(q0, B), :] = l

            def col_panel(j):
                def f():
                    h, l = split(dot3(split(E[j * B : (j + 1) * B, pl.ds(q0, B)]), gq(), NT))
                    LT[j * B : (j + 1) * B, 0:B] = h
                    LT[j * B : (j + 1) * B, B : 2 * B] = l

                return f

            chunks = []
            if with_p:
                chunks += [col_panel(j) for j in range(KB)]
                chunks += [row_panel(c0, 256) for c0 in range(0, PR, 256)]
            return chunks + [r_panel, transposed]

        def trail_chunks():
            def trail(j, c0, w):
                def f():
                    rows = slice(j * B, (j + 1) * B)
                    u = dot(LT[rows, :], RHH[:, c0 : c0 + w], NN)
                    u = u + dot(LT[rows, 0:B], RLO[:, c0 : c0 + w], NN)
                    E[rows, c0 : c0 + w] = E[rows, c0 : c0 + w] - u

                return f

            parts = ((0, 512), (512, 512), (PR, RR))
            return [trail(j, c0, w) for j in range(KB) for c0, w in parts]

        def body(k, carry):
            q = jnp.maximum(k - 1, 0)
            q0 = pl.multiple_of(q * B, B)
            k0 = pl.multiple_of(k * B, B)
            n0 = pl.multiple_of(jnp.minimum(k + 1, KB - 1) * B, B)
            chunks = panel_chunks(q, q0, True) + trail_chunks()
            n = len(chunks)

            def fill(s):
                drain(chunks[n * s // 16 : n * (s + 1) // 16])

            factor128(D, Y, G, LBT, fill)
            y = split(Y[...])
            g = split(G[...])
            lb = split(LBT[...])
            for i in range(2):
                YQ[i] = y[i]
                GQ[i] = g[i]
                LQ[i] = lb[i]
            crit(E, D, y, g, k0, n0)
            return carry

        lax.fori_loop(0, KB, body, 0)
        drain(panel_chunks(KB - 1, (KB - 1) * B, False))
        for k in range(KB - 1, -1, -1):
            rows = slice(k * B, (k + 1) * B)
            v = ZR[rows, :]
            if k < KB - 1:
                later = slice((k + 1) * B, PR)
                v = v - dot3((ZPH[rows, later], ZPL[rows, later]), (VH[later, :], VL[later, :]), NN)
            v = dot3((GTH[rows, :], GTL[rows, :]), split(v), NN)
            h, l = split(v)
            VH[rows, :] = h
            VL[rows, :] = l
            h, l = split(v.T)
            vth[:, rows] = h
            vtl[:, rows] = l
        for p in range(PANELS):
            c0 = pl.multiple_of(cid * BS + p * NB, BS)
            x = XT[pl.ds(c0, BS), :]
            col = c0 + lax.broadcasted_iota(jnp.int32, (BS, RR), 0)
            ln = lax.broadcasted_iota(jnp.int32, (BS, RR), 1)
            x = jnp.where(jnp.logical_and(ln < BS, col > rid * BS + ln), 0.0, x)
            xc[:, BS * p : BS * (p + 1)] = x.T

    vm = pl.BlockSpec(memory_space=pltpu.VMEM)
    V = pltpu.VMEM
    out = jax.ShapeDtypeStruct((RR, PR), bf16)
    return pl.pallas_call(
        kern,
        out_shape=(out, out, jax.ShapeDtypeStruct((RR, PANELS * BS), f32)),
        in_specs=[pl.BlockSpec(memory_space=pltpu.SMEM), pl.BlockSpec(memory_space=pl.ANY)],
        out_specs=(vm, vm, vm),
        scratch_shapes=[
            V((PR, W), f32),
            V((B, B), f32),
            V((B, B), f32),
            V((B, B), f32),
            V((B, B), f32),
            V((2, B, B), bf16),
            V((2, B, B), bf16),
            V((2, B, B), bf16),
            V((PR, 2 * B), bf16),
            V((2 * B, W), bf16),
            V((B, W), bf16),
            V((PR, PR), bf16),
            V((PR, PR), bf16),
            V((PR, RR), f32),
            V((PR, B), bf16),
            V((PR, B), bf16),
            V((PR, RR), bf16),
            V((PR, RR), bf16),
            V((PR, RR), f32),
            pltpu.SemaphoreType.DMA((PANELS * n_col,)),
        ],
        compiler_params=pltpu.CompilerParams(vmem_limit_bytes=40 * 1024 * 1024),
        cost_estimate=pl.CostEstimate(flops=40_000_000_000, bytes_accessed=8_000_000, transcendentals=0),
        name="panel_solve",
    )(ids, gathered)


def trailing_update(vth, vtl, xc, a_cols, local):
    RR, CC = local.shape
    step = 256

    def kern(vth, vtl, xc, ac, al, out):
        out[...] = al[...] - dot3((vth[...], vtl[...]), split(ac[...]), NN)

        @pl.when(pl.program_id(0) == 0)
        def _():
            out[:, 0 : PANELS * BS] = xc[...]

    whole = lambda a: pl.BlockSpec(a.shape, lambda i: (0, 0))
    part = lambda rows: pl.BlockSpec((rows, step), lambda i: (0, i))
    return pl.pallas_call(
        kern,
        grid=(CC // step,),
        out_shape=jax.ShapeDtypeStruct((RR, CC), f32),
        in_specs=[whole(vth), whole(vtl), whole(xc), part(PR), part(RR)],
        out_specs=part(RR),
        compiler_params=pltpu.CompilerParams(vmem_limit_bytes=24 * 1024 * 1024),
        name="trailing_update",
    )(vth, vtl, xc, a_cols, local)


def shards(matrix):
    rid = lax.axis_index(("y", "x"))
    cid = lax.axis_index(("z", "k"))
    ids = jnp.stack([rid, cid]).astype(jnp.int32)
    n_row = lax.axis_size(("y", "x"))
    thin = PANELS * BS
    block = matrix[:BS, :thin].reshape(1, BS * thin // 128, 128)
    block = jnp.broadcast_to(block, (n_row, BS * thin // 128, 128))
    own = lax.all_to_all(block, ("y", "x"), 0, 0, tiled=True).reshape(PR, thin).T
    mine = jnp.concatenate([own, matrix[:, :thin].T], axis=1)
    mine, top = lax.optimization_barrier((mine, matrix[:BS]))
    gathered = lax.all_gather(mine, ("z", "k"), axis=0, tiled=True)
    a_cols = lax.all_gather(top, "x", axis=0, tiled=True)
    a_cols = lax.all_gather(a_cols, "y", axis=0, tiled=True)
    vth, vtl, xc = panel_solve(ids, gathered)
    return trailing_update(vth, vtl, xc, a_cols, matrix)


def solution(mesh):
    four = Mesh(mesh.devices.reshape(8, 4, 8, 2), ("y", "x", "z", "k"))
    placed = P(("y", "x"), ("z", "k"))
    return jax.shard_map(shards, mesh=four, in_specs=(placed,), out_specs=placed, check_vma=False)
```

```python
import jax
import jax.numpy as jnp
from jax import lax
from jax.experimental import pallas as pl
from jax.experimental.pallas import tpu as pltpu
from jax.sharding import Mesh
from jax.sharding import PartitionSpec as P

NB = 512
PANELS = 2
BS = 32
PR = NB * PANELS
B = 128
KB = PR // B
KA = 2

f32 = jnp.float32
bf16 = jnp.bfloat16
NN = (((1,), (0,)), ((), ()))
NT = (((1,), (1,)), ((), ()))


def split(x):
    hi = x.astype(bf16)
    lo = (x - hi.astype(f32)).astype(bf16)
    return hi, lo


def dot(a, b, dims):
    return lax.dot_general(a, b, dims, preferred_element_type=f32)


def dot3(a, b, dims):
    ah, al = a
    bh, bl = b
    return dot(ah, bh, dims) + (dot(ah, bl, dims) + dot(al, bh, dims))


def tree(terms):
    while len(terms) > 1:
        terms = [sum(terms[i : i + 2][1:], terms[i]) for i in range(0, len(terms), 2)]
    return terms[0]


def lane_b(x, lane):
    return jnp.broadcast_to(x[:, lane : lane + 1], (8, 128))


def sub_b(x, row):
    return jnp.broadcast_to(x[row : row + 1, :], (8, 128))


def factor128(d_ref, y_ref, g_ref, lbt_ref, fill):
    row = lax.broadcasted_iota(jnp.int32, (8, 128), 0)
    lane = lax.broadcasted_iota(jnp.int32, (8, 128), 1)
    S = [d_ref[8 * s : 8 * s + 8, :] for s in range(16)]
    G = [jnp.where(lane == row + 8 * s, 1.0, 0.0).astype(f32) for s in range(16)]

    def column(vals):
        for bit in range(3):
            odd = row // (1 << bit) % 2 == 1
            vals = [jnp.where(odd, vals[t + 1], vals[t]) for t in range(0, len(vals), 2)]
        return vals[0]

    for s in range(16):
        c = [lane_b(S[s], 8 * s + m) for m in range(8)]
        a = {(t, m): sub_b(c[m], t) for m in range(8) for t in range(m, 8)}
        M = {}
        d = []
        for i in range(8):
            pivot = a[i, i]
            p = 1.0 / pivot
            d.append(pivot)
            old = {j: a[max(i, j), min(i, j)] for j in range(8) if j != i}
            scaled = {j: old[j] * p for j in old}
            for j in old:
                if j > i:
                    M[j, i] = scaled[j]
            for k in old:
                for j in old:
                    if j == k == i + 1:
                        a[k, j] = a[k, j] - (old[j] * old[j]) * p
                    elif j <= k:
                        a[k, j] = a[k, j] - old[j] * scaled[k]
            for j in old:
                a[max(i, j), min(i, j)] = scaled[j]
            a[i, i] = -p
        w = [column([a[max(t, m), min(t, m)] for t in range(8)]) for m in range(8)]
        YS = tree([w[m] * sub_b(S[s], m) for m in range(8)])
        YG = tree([w[m] * sub_b(G[s], m) for m in range(8)])
        y_ref[8 * s : 8 * s + 8, :] = -YG
        g_ref[8 * s : 8 * s + 8, :] = G[s]
        ys = [sub_b(YS, m) for m in range(8)]
        yg = [sub_b(YG, m) for m in range(8)]
        for r in range(s + 1, 16):
            b = [lane_b(S[r], 8 * s + m) for m in range(8)]
            S[r] = S[r] + tree([b[m] * ys[m] for m in range(8)])
            G[r] = G[r] + tree([b[m] * yg[m] for m in range(8)])
        sq = [jnp.sqrt(d[i]) for i in range(8)]
        zero = jnp.zeros((8, 128), f32)
        lb = zero
        for t in range(8):
            vals = [M[t, i] * sq[i] for i in range(t)] + [sq[t]] + [zero] * (7 - t)
            lb = jnp.where(lane == 8 * s + t, column(vals), lb)
        lbt_ref[8 * s : 8 * s + 8, :] = lb
        fill(s)


def drain(chunks):
    for f in chunks:
        f()


def crit(E, D, Y, G, k0, n0):
    zp = split(dot3(Y, split(E[pl.ds(k0, B), pl.ds(n0, B)]), NN))
    zt = split(dot3(split(E[pl.ds(n0, B), pl.ds(k0, B)]), G, NT))
    D[...] = E[pl.ds(n0, B), pl.ds(n0, B)] - dot3(zt, zp, NN)


def first_blocks(a0):
    N = KA * B

    def kern(a_ref, y0, g0, lbt0, E, D, LT, RHH, RLO):
        E[...] = a_ref[0:N, :]
        D[...] = E[0:B, 0:B]
        for k in range(KA):
            rows = slice(k * B, (k + 1) * B)

            def fill(s, k=k):
                if k == 0 or s % 4 or s // 4 >= KA - k:
                    return
                j = k + s // 4
                u = dot(LT[j * B : (j + 1) * B, :], RHH[:, k * B : N], NN)
                u = u + dot(LT[j * B : (j + 1) * B, 0:B], RLO[:, k * B : N], NN)
                E[j * B : (j + 1) * B, k * B : N] = E[j * B : (j + 1) * B, k * B : N] - u

            factor128(D, y0.at[rows, :], g0.at[rows, :], lbt0.at[rows, :], fill)
            if k < KA - 1:
                y = split(y0[rows, :])
                g = split(g0[rows, :])
                crit(E, D, y, g, k * B, (k + 1) * B)
                h, l = split(dot3(y, split(E[rows, (k + 1) * B : N]), NN))
                RHH[0:B, (k + 1) * B : N] = h
                RHH[B : 2 * B, (k + 1) * B : N] = h
                RLO[:, (k + 1) * B : N] = l
                h, l = split(dot3(split(E[(k + 1) * B : N, rows]), g, NT))
                LT[(k + 1) * B : N, 0:B] = h
                LT[(k + 1) * B : N, B : 2 * B] = l

    vm = pl.BlockSpec(memory_space=pltpu.VMEM)
    V = pltpu.VMEM
    out = jax.ShapeDtypeStruct((N, B), f32)
    return pl.pallas_call(
        kern,
        out_shape=(out, out, out),
        in_specs=[vm],
        out_specs=(vm, vm, vm),
        scratch_shapes=[V((N, N), f32), V((B, B), f32), V((N, 2 * B), bf16), V((2 * B, N), bf16), V((B, N), bf16)],
        compiler_params=pltpu.CompilerParams(vmem_limit_bytes=24 * 1024 * 1024),
        cost_estimate=pl.CostEstimate(flops=15_000_000_000, bytes_accessed=2_000_000, transcendentals=0),
        name="first_blocks",
    )(a0)


def panel_solve(ids, gathered, y0, g0, lbt0):
    W = gathered.shape[1]
    RR = W - PR
    n_col = PR // (PANELS * BS)

    def kern(id_ref, pr_ref, y0, g0, lbt0, vth, vtl, xc, E, D, Y, G, LBT, YQ, GQ, LQ, LT, RHH, RLO, ZPH, ZPL, LRH, LRL, XT, sems):
        copies = []
        for c in range(n_col):
            for p in range(PANELS):
                n = c * PANELS + p
                copies.append(
                    pltpu.make_async_copy(
                        pr_ref.at[pl.ds(n * BS, BS), :], E.at[pl.ds(p * NB + c * BS, BS), :], sems.at[n]
                    )
                )
        for copy in copies:
            copy.start()
        for copy in copies:
            copy.wait()
        rid = id_ref[0]
        cid = id_ref[1]
        second = rid >= NB // BS
        lane_r = lax.broadcasted_iota(jnp.int32, (B, RR), 1)

        def panel_chunks(q, q0, first):
            def yq():
                return YQ[0], YQ[1]

            def gq():
                return GQ[0], GQ[1]

            def keep(c0, w, h, l):
                RHH[0:B, c0 : c0 + w] = h
                RHH[B : 2 * B, c0 : c0 + w] = h
                RLO[:, c0 : c0 + w] = l

            def row_panel(c0, w):
                def f():
                    h, l = split(dot3(yq(), split(E[pl.ds(q0, B), c0 : c0 + w]), NN))
                    keep(c0, w, h, l)
                    ZPH[pl.ds(q0, B), c0 : c0 + w] = h
                    ZPL[pl.ds(q0, B), c0 : c0 + w] = l

                return f

            def pivot_columns():
                h, l = yq()
                RHH[0:B, pl.ds(q0, B)] = h
                RHH[B : 2 * B, pl.ds(q0, B)] = h
                RLO[:, pl.ds(q0, B)] = l
                ZPH[pl.ds(q0, B), pl.ds(q0, B)] = h
                ZPL[pl.ds(q0, B), pl.ds(q0, B)] = l
                E[first * B : PR, pl.ds(q0, B)] = jnp.zeros((PR - first * B, B), f32)

            def r_panel():
                e = split(E[pl.ds(q0, B), PR:W])
                zp = split(dot3(yq(), e, NN))
                keep(PR, RR, *zp)
                XT[pl.ds(q0, B), :] = dot3((LQ[0], LQ[1]), zp, NN)
                z = dot3(gq(), e, NN)
                live = jnp.logical_and(second, q < NB // B)
                z = jnp.where(jnp.logical_and(lane_r < BS, jnp.logical_not(live)), 0.0, z)
                h, l = split(z.T)
                LRH[:, pl.ds(q0, B)] = h
                LRL[:, pl.ds(q0, B)] = l

            def last_pivot():
                ZPH[pl.ds(q0, B), pl.ds(q0, B)] = YQ[0]
                ZPL[pl.ds(q0, B), pl.ds(q0, B)] = YQ[1]

            def col_panel(j):
                def f():
                    h, l = split(dot3(split(E[j * B : (j + 1) * B, pl.ds(q0, B)]), gq(), NT))
                    LT[j * B : (j + 1) * B, 0:B] = h
                    LT[j * B : (j + 1) * B, B : 2 * B] = l

                return f

            chunks = []
            chunks += [col_panel(j) for j in range(first, KB)]
            chunks += [row_panel(c0, 256) for c0 in range(0, PR, 256)]
            return chunks + [pivot_columns, r_panel] if first < KB else chunks + [last_pivot, r_panel]

        def trail_chunks(first):
            def trail(j, c0, w):
                def f():
                    rows = slice(j * B, (j + 1) * B)
                    u = dot(LT[rows, :], RHH[:, c0 : c0 + w], NN)
                    u = u + dot(LT[rows, 0:B], RLO[:, c0 : c0 + w], NN)
                    E[rows, c0 : c0 + w] = E[rows, c0 : c0 + w] - u

                return f

            parts = [(c0, 512) for c0 in range(0, PR, 512)] + [(PR, RR)]
            return [trail(j, c0, w) for j in range(first, KB) for c0, w in parts]

        for k in range(KA):
            rows = slice(k * B, (k + 1) * B)
            for q_ref, ref in ((YQ, y0), (GQ, g0), (LQ, lbt0)):
                q_ref[0], q_ref[1] = split(ref[rows, :])
            if k < KA - 1:
                drain(panel_chunks(k, k * B, k + 1) + trail_chunks(k + 1))
        crit(E, D, (YQ[0], YQ[1]), (GQ[0], GQ[1]), (KA - 1) * B, KA * B)

        def body(k, carry):
            q = k - 1
            q0 = pl.multiple_of(q * B, B)
            k0 = pl.multiple_of(k * B, B)
            n0 = pl.multiple_of(jnp.minimum(k + 1, KB - 1) * B, B)
            chunks = panel_chunks(q, q0, KA) + trail_chunks(KA)
            n = len(chunks)

            def fill(s):
                drain(chunks[n * s // 16 : n * (s + 1) // 16])

            factor128(D, Y, G, LBT, fill)
            y = split(Y[...])
            g = split(G[...])
            lb = split(LBT[...])
            for i in range(2):
                YQ[i] = y[i]
                GQ[i] = g[i]
                LQ[i] = lb[i]
            crit(E, D, y, g, k0, n0)
            return carry

        lax.fori_loop(KA, KB, body, 0)
        drain(panel_chunks(KB - 1, (KB - 1) * B, KB))
        for c0 in range(0, PR, 256):
            for ref in (ZPH, ZPL):
                ref[c0 : c0 + B, c0 + B : c0 + 2 * B] = jnp.zeros((B, B), bf16)
            z = (ZPH[c0:PR, c0 : c0 + 256], ZPL[c0:PR, c0 : c0 + 256])
            h, l = split(dot3((LRH[:, c0:PR], LRL[:, c0:PR]), z, NN))
            vth[:, c0 : c0 + 256] = h
            vtl[:, c0 : c0 + 256] = l
        for p in range(PANELS):
            c0 = pl.multiple_of(cid * BS + p * NB, BS)
            x = XT[pl.ds(c0, BS), :]
            col = c0 + lax.broadcasted_iota(jnp.int32, (BS, RR), 0)
            ln = lax.broadcasted_iota(jnp.int32, (BS, RR), 1)
            x = jnp.where(jnp.logical_and(ln < BS, col > rid * BS + ln), 0.0, x)
            xc[:, BS * p : BS * (p + 1)] = x.T

    vm = pl.BlockSpec(memory_space=pltpu.VMEM)
    V = pltpu.VMEM
    out = jax.ShapeDtypeStruct((RR, PR), bf16)
    return pl.pallas_call(
        kern,
        out_shape=(out, out, jax.ShapeDtypeStruct((RR, PANELS * BS), f32)),
        in_specs=[pl.BlockSpec(memory_space=pltpu.SMEM), pl.BlockSpec(memory_space=pl.ANY), vm, vm, vm],
        out_specs=(vm, vm, vm),
        scratch_shapes=[
            V((PR, W), f32),
            V((B, B), f32),
            V((B, B), f32),
            V((B, B), f32),
            V((B, B), f32),
            V((2, B, B), bf16),
            V((2, B, B), bf16),
            V((2, B, B), bf16),
            V((PR, 2 * B), bf16),
            V((2 * B, W), bf16),
            V((B, W), bf16),
            V((PR, PR), bf16),
            V((PR, PR), bf16),
            V((RR, PR), bf16),
            V((RR, PR), bf16),
            V((PR, RR), f32),
            pltpu.SemaphoreType.DMA((PANELS * n_col,)),
        ],
        compiler_params=pltpu.CompilerParams(vmem_limit_bytes=58 * 1024 * 1024),
        cost_estimate=pl.CostEstimate(flops=30_000_000_000, bytes_accessed=8_000_000, transcendentals=0),
        name="panel_solve",
    )(ids, gathered, y0, g0, lbt0)


def trailing_update(vth, vtl, xc, a_cols, local):
    RR, CC = local.shape
    step = 256

    def kern(vth, vtl, xc, ac, al, out):
        out[...] = al[...] - dot3((vth[...], vtl[...]), split(ac[...]), NN)

        @pl.when(pl.program_id(0) == 0)
        def _():
            out[:, 0 : PANELS * BS] = xc[...]

    whole = lambda a: pl.BlockSpec(a.shape, lambda i: (0, 0))
    part = lambda rows: pl.BlockSpec((rows, step), lambda i: (0, i))
    return pl.pallas_call(
        kern,
        grid=(CC // step,),
        out_shape=jax.ShapeDtypeStruct((RR, CC), f32),
        in_specs=[whole(vth), whole(vtl), whole(xc), part(PR), part(RR)],
        out_specs=part(RR),
        compiler_params=pltpu.CompilerParams(vmem_limit_bytes=58 * 1024 * 1024),
        name="trailing_update",
    )(vth, vtl, xc, a_cols, local)


def shards(matrix):
    rid = lax.axis_index(("y", "x"))
    cid = lax.axis_index(("z", "k"))
    ids = jnp.stack([rid, cid]).astype(jnp.int32)
    n_row = lax.axis_size(("y", "x"))
    thin = PANELS * BS
    block = matrix[:BS, :thin].reshape(1, BS * thin // 128, 128)
    block = jnp.broadcast_to(block, (n_row, BS * thin // 128, 128))
    own = lax.all_to_all(block, ("y", "x"), 0, 0, tiled=True).reshape(PR, thin).T
    mine = jnp.concatenate([own, matrix[:, :thin].T], axis=1)
    early = own[:BS, : KA * B]
    mine, early = lax.optimization_barrier((mine, early))
    gathered = lax.all_gather(mine, ("z", "k"), axis=0, tiled=True)
    early = lax.all_gather(early, ("z", "k"), axis=0, tiled=True)
    early, top = lax.optimization_barrier((early, matrix[:BS]))
    top = lax.all_gather(top, "x", axis=0, tiled=True)
    early, top = lax.optimization_barrier((early, top))
    factors = first_blocks(early)
    a_cols = lax.all_gather(top, "y", axis=0, tiled=True)
    vth, vtl, xc = panel_solve(ids, gathered, *factors)
    return trailing_update(vth, vtl, xc, a_cols, matrix)


def solution(mesh):
    four = Mesh(mesh.devices.reshape(8, 4, 8, 2), ("y", "x", "z", "k"))
    placed = P(("y", "x"), ("z", "k"))
    return jax.shard_map(shards, mesh=four, in_specs=(placed,), out_specs=placed, check_vma=False)
```

```python
import jax
import jax.numpy as jnp
from jax import lax
from jax.experimental import pallas as pl
from jax.experimental.pallas import tpu as pltpu
from jax.sharding import Mesh
from jax.sharding import PartitionSpec as P

NB = 512
PANELS = 2
BS = 32
PR = NB * PANELS
B = 128
KB = PR // B
KA = 3

f32 = jnp.float32
bf16 = jnp.bfloat16
NN = (((1,), (0,)), ((), ()))
NT = (((1,), (1,)), ((), ()))


def split(x):
    hi = x.astype(bf16)
    lo = (x - hi.astype(f32)).astype(bf16)
    return hi, lo


def dot(a, b, dims):
    return lax.dot_general(a, b, dims, preferred_element_type=f32)


def dot3(a, b, dims):
    ah, al = a
    bh, bl = b
    return dot(ah, bh, dims) + (dot(ah, bl, dims) + dot(al, bh, dims))


def tree(terms):
    while len(terms) > 1:
        terms = [sum(terms[i : i + 2][1:], terms[i]) for i in range(0, len(terms), 2)]
    return terms[0]


def lane_b(x, lane):
    return jnp.broadcast_to(x[:, lane : lane + 1], (8, 128))


def sub_b(x, row):
    return jnp.broadcast_to(x[row : row + 1, :], (8, 128))


def factor128(d_ref, y_ref, g_ref, lbt_ref, fill):
    row = lax.broadcasted_iota(jnp.int32, (8, 128), 0)
    lane = lax.broadcasted_iota(jnp.int32, (8, 128), 1)
    S = [d_ref[8 * s : 8 * s + 8, :] for s in range(16)]
    G = [jnp.where(lane == row + 8 * s, 1.0, 0.0).astype(f32) for s in range(16)]

    def column(vals):
        for bit in range(3):
            odd = row // (1 << bit) % 2 == 1
            vals = [jnp.where(odd, vals[t + 1], vals[t]) for t in range(0, len(vals), 2)]
        return vals[0]

    c = [lane_b(S[0], m) for m in range(8)]
    for s in range(16):
        if s < 15:
            near = [lane_b(S[s + 1], 8 * s + m) for m in range(8)]
            ahead = [lane_b(S[s + 1], 8 * s + 8 + m) for m in range(8)]
        a = {(t, m): sub_b(c[m], t) for m in range(8) for t in range(m, 8)}
        M = {}
        d = []
        for i in range(8):
            pivot = a[i, i]
            p = 1.0 / pivot
            d.append(pivot)
            old = {j: a[max(i, j), min(i, j)] for j in range(8) if j != i}
            scaled = {j: old[j] * p for j in old}
            for j in old:
                if j > i:
                    M[j, i] = scaled[j]
            for k in old:
                for j in old:
                    if j == k == i + 1:
                        a[k, j] = a[k, j] - (old[j] * old[j]) * p
                    elif j <= k:
                        a[k, j] = a[k, j] - old[j] * scaled[k]
            for j in old:
                a[max(i, j), min(i, j)] = scaled[j]
            a[i, i] = -p
        if s < 15:
            R = [tree([a[max(i, j), min(i, j)] * near[j] for j in range(8)]) for i in range(8)]
            c = [ahead[m] + tree([near[i] * sub_b(R[i], m) for i in range(8)]) for m in range(8)]
        w = [column([a[max(t, m), min(t, m)] for t in range(8)]) for m in range(8)]
        YS = tree([w[m] * sub_b(S[s], m) for m in range(8)])
        YG = tree([w[m] * sub_b(G[s], m) for m in range(8)])
        y_ref[8 * s : 8 * s + 8, :] = -YG
        g_ref[8 * s : 8 * s + 8, :] = G[s]
        ys = [sub_b(YS, m) for m in range(8)]
        yg = [sub_b(YG, m) for m in range(8)]
        for r in range(s + 1, 16):
            b = near if r == s + 1 else [lane_b(S[r], 8 * s + m) for m in range(8)]
            S[r] = S[r] + tree([b[m] * ys[m] for m in range(8)])
            G[r] = G[r] + tree([b[m] * yg[m] for m in range(8)])
        sq = [jnp.sqrt(d[i]) for i in range(8)]
        zero = jnp.zeros((8, 128), f32)
        lb = zero
        for t in range(8):
            vals = [M[t, i] * sq[i] for i in range(t)] + [sq[t]] + [zero] * (7 - t)
            lb = jnp.where(lane == 8 * s + t, column(vals), lb)
        lbt_ref[8 * s : 8 * s + 8, :] = lb
        fill(s)


def drain(chunks):
    for f in chunks:
        f()


def crit(E, D, Y, G, k0, n0):
    zp = split(dot3(Y, split(E[pl.ds(k0, B), pl.ds(n0, B)]), NN))
    zt = split(dot3(split(E[pl.ds(n0, B), pl.ds(k0, B)]), G, NT))
    D[...] = E[pl.ds(n0, B), pl.ds(n0, B)] - dot3(zt, zp, NN)


def first_blocks(a0):
    N = KA * B

    def kern(a_ref, f0, E, D, LT, RHH, RLO):
        E[...] = a_ref[0:N, :]
        D[...] = E[0:B, 0:B]
        for k in range(KA):
            rows = slice(k * B, (k + 1) * B)

            def fill(s, k=k):
                if k == 0 or s % 4 or s // 4 >= KA - k:
                    return
                j = k + s // 4
                u = dot(LT[j * B : (j + 1) * B, :], RHH[:, k * B : N], NN)
                u = u + dot(LT[j * B : (j + 1) * B, 0:B], RLO[:, k * B : N], NN)
                E[j * B : (j + 1) * B, k * B : N] = E[j * B : (j + 1) * B, k * B : N] - u

            y0, g0, lbt0 = (f0.at[n * N + k * B : n * N + (k + 1) * B, :] for n in range(3))
            factor128(D, y0, g0, lbt0, fill)
            if k < KA - 1:
                y = split(y0[...])
                g = split(g0[...])
                crit(E, D, y, g, k * B, (k + 1) * B)
                h, l = split(dot3(y, split(E[rows, (k + 1) * B : N]), NN))
                RHH[0:B, (k + 1) * B : N] = h
                RHH[B : 2 * B, (k + 1) * B : N] = h
                RLO[:, (k + 1) * B : N] = l
                h, l = split(dot3(split(E[(k + 1) * B : N, rows]), g, NT))
                LT[(k + 1) * B : N, 0:B] = h
                LT[(k + 1) * B : N, B : 2 * B] = l

    vm = pl.BlockSpec(memory_space=pltpu.VMEM)
    V = pltpu.VMEM
    return pl.pallas_call(
        kern,
        out_shape=jax.ShapeDtypeStruct((3 * N, B), f32),
        in_specs=[vm],
        out_specs=vm,
        scratch_shapes=[V((N, N), f32), V((B, B), f32), V((N, 2 * B), bf16), V((2 * B, N), bf16), V((B, N), bf16)],
        compiler_params=pltpu.CompilerParams(vmem_limit_bytes=24 * 1024 * 1024),
        cost_estimate=pl.CostEstimate(flops=17_000_000_000, bytes_accessed=2_000_000, transcendentals=0),
        name="first_blocks",
    )(a0)


def panel_solve(ids, gathered, factors):
    W = gathered.shape[1]
    RR = W - PR
    n_col = PR // (PANELS * BS)

    def kern(id_ref, pr_ref, f0, vth, vtl, xc, E, D, Y, G, LBT, YQ, GQ, LQ, LT, RHH, RLO, ZPH, ZPL, LRH, LRL, XT, sems):
        copies = []
        for p in range(PANELS):
            for c in range(n_col):
                n = c * PANELS + p
                copies.append(
                    pltpu.make_async_copy(
                        pr_ref.at[pl.ds(n * BS, BS), :], E.at[pl.ds(p * NB + c * BS, BS), :], sems.at[n]
                    )
                )
        for copy in copies:
            copy.start()
        for copy in copies[: B // BS]:
            copy.wait()
        rid = id_ref[0]
        cid = id_ref[1]
        second = rid >= NB // BS
        lane_r = lax.broadcasted_iota(jnp.int32, (B, RR), 1)

        def panel_chunks(q, q0, first):
            def yq():
                return YQ[0], YQ[1]

            def gq():
                return GQ[0], GQ[1]

            def keep(c0, w, h, l):
                RHH[0:B, c0 : c0 + w] = h
                RHH[B : 2 * B, c0 : c0 + w] = h
                RLO[:, c0 : c0 + w] = l

            def row_panel(c0, w):
                def f():
                    h, l = split(dot3(yq(), split(E[pl.ds(q0, B), c0 : c0 + w]), NN))
                    keep(c0, w, h, l)
                    ZPH[pl.ds(q0, B), c0 : c0 + w] = h
                    ZPL[pl.ds(q0, B), c0 : c0 + w] = l

                return f

            def pivot_columns():
                h, l = yq()
                RHH[0:B, pl.ds(q0, B)] = h
                RHH[B : 2 * B, pl.ds(q0, B)] = h
                RLO[:, pl.ds(q0, B)] = l
                ZPH[pl.ds(q0, B), pl.ds(q0, B)] = h
                ZPL[pl.ds(q0, B), pl.ds(q0, B)] = l
                E[first * B : PR, pl.ds(q0, B)] = jnp.zeros((PR - first * B, B), f32)

            def r_panel():
                e = split(E[pl.ds(q0, B), PR:W])
                zp = split(dot3(yq(), e, NN))
                keep(PR, RR, *zp)
                XT[pl.ds(q0, B), :] = dot3((LQ[0], LQ[1]), zp, NN)
                z = dot3(gq(), e, NN)
                live = jnp.logical_and(second, q < NB // B)
                z = jnp.where(jnp.logical_and(lane_r < BS, jnp.logical_not(live)), 0.0, z)
                h, l = split(z.T)
                LRH[:, pl.ds(q0, B)] = h
                LRL[:, pl.ds(q0, B)] = l

            def last_pivot():
                ZPH[pl.ds(q0, B), pl.ds(q0, B)] = YQ[0]
                ZPL[pl.ds(q0, B), pl.ds(q0, B)] = YQ[1]

            def col_panel(j):
                def f():
                    h, l = split(dot3(split(E[j * B : (j + 1) * B, pl.ds(q0, B)]), gq(), NT))
                    LT[j * B : (j + 1) * B, 0:B] = h
                    LT[j * B : (j + 1) * B, B : 2 * B] = l

                return f

            chunks = []
            chunks += [col_panel(j) for j in range(first, KB)]
            chunks += [row_panel(c0, 256) for c0 in range(0, PR, 256)]
            return chunks + [pivot_columns, r_panel] if first < KB else chunks + [last_pivot, r_panel]

        def trail_chunks(first):
            def trail(j, c0, w):
                def f():
                    rows = slice(j * B, (j + 1) * B)
                    u = dot(LT[rows, :], RHH[:, c0 : c0 + w], NN)
                    u = u + dot(LT[rows, 0:B], RLO[:, c0 : c0 + w], NN)
                    E[rows, c0 : c0 + w] = E[rows, c0 : c0 + w] - u

                return f

            parts = [(c0, 512) for c0 in range(0, PR, 512)] + [(PR, RR)]
            return [trail(j, c0, w) for j in range(first, KB) for c0, w in parts]

        for k in range(KA):
            for n, ref in enumerate((YQ, GQ, LQ)):
                ref[0], ref[1] = split(f0[(n * KA + k) * B : (n * KA + k + 1) * B, :])
            if k == 0:
                chunks = panel_chunks(k, k * B, k + 1)
                drain(chunks[KB - 1 : KB + 3])
                for copy in copies[B // BS :]:
                    copy.wait()
                drain(chunks[: KB - 1] + chunks[KB + 3 :] + trail_chunks(k + 1))
            elif k < KA - 1:
                drain(panel_chunks(k, k * B, k + 1) + trail_chunks(k + 1))
        crit(E, D, (YQ[0], YQ[1]), (GQ[0], GQ[1]), (KA - 1) * B, KA * B)

        def body(k, carry):
            q = k - 1
            q0 = pl.multiple_of(q * B, B)
            k0 = pl.multiple_of(k * B, B)
            n0 = pl.multiple_of(jnp.minimum(k + 1, KB - 1) * B, B)
            chunks = panel_chunks(q, q0, KA) + trail_chunks(KA)
            n = len(chunks)

            def fill(s):
                drain(chunks[n * s // 16 : n * (s + 1) // 16])

            factor128(D, Y, G, LBT, fill)
            y = split(Y[...])
            g = split(G[...])
            lb = split(LBT[...])
            for i in range(2):
                YQ[i] = y[i]
                GQ[i] = g[i]
                LQ[i] = lb[i]
            crit(E, D, y, g, k0, n0)
            return carry

        lax.fori_loop(KA, KB, body, 0)
        drain(panel_chunks(KB - 1, (KB - 1) * B, KB))
        for c0 in range(0, PR, 256):
            for ref in (ZPH, ZPL):
                ref[c0 : c0 + B, c0 + B : c0 + 2 * B] = jnp.zeros((B, B), bf16)
            z = (ZPH[c0:PR, c0 : c0 + 256], ZPL[c0:PR, c0 : c0 + 256])
            h, l = split(dot3((LRH[:, c0:PR], LRL[:, c0:PR]), z, NN))
            vth[:, c0 : c0 + 256] = h
            vtl[:, c0 : c0 + 256] = l
        for p in range(PANELS):
            c0 = pl.multiple_of(cid * BS + p * NB, BS)
            x = XT[pl.ds(c0, BS), :]
            col = c0 + lax.broadcasted_iota(jnp.int32, (BS, RR), 0)
            ln = lax.broadcasted_iota(jnp.int32, (BS, RR), 1)
            x = jnp.where(jnp.logical_and(ln < BS, col > rid * BS + ln), 0.0, x)
            xc[:, BS * p : BS * (p + 1)] = x.T

    vm = pl.BlockSpec(memory_space=pltpu.VMEM)
    V = pltpu.VMEM
    out = jax.ShapeDtypeStruct((RR, PR), bf16)
    return pl.pallas_call(
        kern,
        out_shape=(out, out, jax.ShapeDtypeStruct((RR, PANELS * BS), f32)),
        in_specs=[pl.BlockSpec(memory_space=pltpu.SMEM), pl.BlockSpec(memory_space=pl.ANY), vm],
        out_specs=(vm, vm, vm),
        scratch_shapes=[
            V((PR, W), f32),
            V((B, B), f32),
            V((B, B), f32),
            V((B, B), f32),
            V((B, B), f32),
            V((2, B, B), bf16),
            V((2, B, B), bf16),
            V((2, B, B), bf16),
            V((PR, 2 * B), bf16),
            V((2 * B, W), bf16),
            V((B, W), bf16),
            V((PR, PR), bf16),
            V((PR, PR), bf16),
            V((RR, PR), bf16),
            V((RR, PR), bf16),
            V((PR, RR), f32),
            pltpu.SemaphoreType.DMA((PANELS * n_col,)),
        ],
        compiler_params=pltpu.CompilerParams(vmem_limit_bytes=58 * 1024 * 1024),
        cost_estimate=pl.CostEstimate(flops=46_000_000_000, bytes_accessed=8_000_000, transcendentals=0),
        name="panel_solve",
    )(ids, gathered, factors)


def trailing_update(vth, vtl, xc, a_cols, local):
    RR, CC = local.shape
    step = 256

    def kern(vth, vtl, xc, ac, al, out):
        out[...] = al[...] - dot3((vth[...], vtl[...]), split(ac[...]), NN)

        @pl.when(pl.program_id(0) == 0)
        def _():
            out[:, 0 : PANELS * BS] = xc[...]

    whole = lambda a: pl.BlockSpec(a.shape, lambda i: (0, 0))
    part = lambda rows: pl.BlockSpec((rows, step), lambda i: (0, i))
    return pl.pallas_call(
        kern,
        grid=(CC // step,),
        out_shape=jax.ShapeDtypeStruct((RR, CC), f32),
        in_specs=[whole(vth), whole(vtl), whole(xc), part(PR), part(RR)],
        out_specs=part(RR),
        compiler_params=pltpu.CompilerParams(vmem_limit_bytes=62 * 1024 * 1024),
        name="trailing_update",
    )(vth, vtl, xc, a_cols, local)


def shards(matrix):
    rid = lax.axis_index(("y", "x"))
    cid = lax.axis_index(("z", "k"))
    ids = jnp.stack([rid, cid]).astype(jnp.int32)
    n_row = lax.axis_size(("y", "x"))
    thin = PANELS * BS
    block = matrix[:BS, :thin].reshape(1, BS * thin // 128, 128)
    block = jnp.broadcast_to(block, (n_row, BS * thin // 128, 128))
    own = lax.all_to_all(block, ("y", "x"), 0, 0, tiled=True).reshape(PR, thin).T
    mine = jnp.concatenate([own, matrix[:, :thin].T], axis=1)
    early = own[:BS, : KA * B]
    mine, early, top = lax.optimization_barrier((mine, early, matrix[:BS]))
    top = jnp.broadcast_to(top[None], (n_row,) + top.shape)
    a_cols = lax.all_to_all(top, ("y", "x"), 0, 0, tiled=True).reshape(PR, top.shape[2])
    gathered = lax.all_gather(mine, ("z", "k"), axis=0, tiled=True)
    early = lax.all_gather(early, ("z", "k"), axis=0, tiled=True)
    factors = first_blocks(early)
    vth, vtl, xc = panel_solve(ids, gathered, factors)
    return trailing_update(vth, vtl, xc, a_cols, matrix)


def solution(mesh):
    four = Mesh(mesh.devices.reshape(8, 4, 8, 2), ("y", "x", "z", "k"))
    placed = P(("y", "x"), ("z", "k"))
    return jax.shard_map(shards, mesh=four, in_specs=(placed,), out_specs=placed, check_vma=False)
```

```python
import jax
import jax.numpy as jnp
from jax import lax
from jax.experimental import pallas as pl
from jax.experimental.pallas import tpu as pltpu
from jax.sharding import Mesh
from jax.sharding import PartitionSpec as P

NB = 512
PANELS = 2
BS = 32
PR = NB * PANELS
B = 128
KB = PR // B
KA = 3

f32 = jnp.float32
bf16 = jnp.bfloat16
NN = (((1,), (0,)), ((), ()))
NT = (((1,), (1,)), ((), ()))


def split(x):
    hi = x.astype(bf16)
    lo = (x - hi.astype(f32)).astype(bf16)
    return hi, lo


def dot(a, b, dims):
    return lax.dot_general(a, b, dims, preferred_element_type=f32)


def dot3(a, b, dims):
    ah, al = a
    bh, bl = b
    return dot(ah, bh, dims) + (dot(ah, bl, dims) + dot(al, bh, dims))


def tree(terms):
    while len(terms) > 1:
        terms = [sum(terms[i : i + 2][1:], terms[i]) for i in range(0, len(terms), 2)]
    return terms[0]


def lane_b(x, lane):
    return jnp.broadcast_to(x[:, lane : lane + 1], (8, 128))


def sub_b(x, row):
    return jnp.broadcast_to(x[row : row + 1, :], (8, 128))


def factor128(d_ref, y_ref, g_ref, lbt_ref, fill):
    row = lax.broadcasted_iota(jnp.int32, (8, 128), 0)
    lane = lax.broadcasted_iota(jnp.int32, (8, 128), 1)
    S = [d_ref[8 * s : 8 * s + 8, :] for s in range(16)]
    G = [jnp.where(lane == row + 8 * s, 1.0, 0.0).astype(f32) for s in range(16)]

    def column(vals):
        for bit in range(3):
            odd = row // (1 << bit) % 2 == 1
            vals = [jnp.where(odd, vals[t + 1], vals[t]) for t in range(0, len(vals), 2)]
        return vals[0]

    c = [lane_b(S[0], m) for m in range(8)]
    for s in range(16):
        if s < 15:
            near = [lane_b(S[s + 1], 8 * s + m) for m in range(8)]
            ahead = [lane_b(S[s + 1], 8 * s + 8 + m) for m in range(8)]
        a = {(t, m): sub_b(c[m], t) for m in range(8) for t in range(m, 8)}
        M = {}
        d = []
        for i in range(8):
            pivot = a[i, i]
            p = 1.0 / pivot
            d.append(pivot)
            old = {j: a[max(i, j), min(i, j)] for j in range(8) if j != i}
            scaled = {j: old[j] * p for j in old}
            for j in old:
                if j > i:
                    M[j, i] = scaled[j]
            for k in old:
                for j in old:
                    if j == k == i + 1:
                        a[k, j] = a[k, j] - (old[j] * old[j]) * p
                    elif j <= k:
                        a[k, j] = a[k, j] - old[j] * scaled[k]
            for j in old:
                a[max(i, j), min(i, j)] = scaled[j]
            a[i, i] = -p
        if s < 15:
            R = [tree([a[max(i, j), min(i, j)] * near[j] for j in range(8)]) for i in range(8)]
            c = [ahead[m] + tree([near[i] * sub_b(R[i], m) for i in range(8)]) for m in range(8)]
        w = [column([a[max(t, m), min(t, m)] for t in range(8)]) for m in range(8)]
        YS = tree([w[m] * sub_b(S[s], m) for m in range(8)])
        YG = tree([w[m] * sub_b(G[s], m) for m in range(8)])
        y_ref[8 * s : 8 * s + 8, :] = -YG
        g_ref[8 * s : 8 * s + 8, :] = G[s]
        ys = [sub_b(YS, m) for m in range(8)]
        yg = [sub_b(YG, m) for m in range(8)]
        for r in range(s + 1, 16):
            b = near if r == s + 1 else [lane_b(S[r], 8 * s + m) for m in range(8)]
            S[r] = S[r] + tree([b[m] * ys[m] for m in range(8)])
            G[r] = G[r] + tree([b[m] * yg[m] for m in range(8)])
        sq = [jnp.sqrt(d[i]) for i in range(8)]
        zero = jnp.zeros((8, 128), f32)
        lb = zero
        for t in range(8):
            vals = [M[t, i] * sq[i] for i in range(t)] + [sq[t]] + [zero] * (7 - t)
            lb = jnp.where(lane == 8 * s + t, column(vals), lb)
        lbt_ref[8 * s : 8 * s + 8, :] = lb
        fill(s)


def drain(chunks):
    for f in chunks:
        f()


def crit(E, D, Y, G, k0, n0):
    zp = split(dot3(Y, split(E[pl.ds(k0, B), pl.ds(n0, B)]), NN))
    zt = split(dot3(split(E[pl.ds(n0, B), pl.ds(k0, B)]), G, NT))
    D[...] = E[pl.ds(n0, B), pl.ds(n0, B)] - dot3(zt, zp, NN)


def first_blocks(a0):
    N = KA * B

    def kern(a_ref, f0, E, D, LT, RHH, RLO):
        E[...] = a_ref[0:N, :]
        D[...] = E[0:B, 0:B]
        for k in range(KA):
            rows = slice(k * B, (k + 1) * B)

            def fill(s, k=k):
                if k == 0 or s % 4 or s // 4 >= KA - k:
                    return
                j = k + s // 4
                u = dot(LT[j * B : (j + 1) * B, :], RHH[:, k * B : N], NN)
                u = u + dot(LT[j * B : (j + 1) * B, 0:B], RLO[:, k * B : N], NN)
                E[j * B : (j + 1) * B, k * B : N] = E[j * B : (j + 1) * B, k * B : N] - u

            y0, g0, lbt0 = (f0.at[n * N + k * B : n * N + (k + 1) * B, :] for n in range(3))
            factor128(D, y0, g0, lbt0, fill)
            if k < KA - 1:
                y = split(y0[...])
                g = split(g0[...])
                crit(E, D, y, g, k * B, (k + 1) * B)
                h, l = split(dot3(y, split(E[rows, (k + 1) * B : N]), NN))
                RHH[0:B, (k + 1) * B : N] = h
                RHH[B : 2 * B, (k + 1) * B : N] = h
                RLO[:, (k + 1) * B : N] = l
                h, l = split(dot3(split(E[(k + 1) * B : N, rows]), g, NT))
                LT[(k + 1) * B : N, 0:B] = h
                LT[(k + 1) * B : N, B : 2 * B] = l

    vm = pl.BlockSpec(memory_space=pltpu.VMEM)
    V = pltpu.VMEM
    return pl.pallas_call(
        kern,
        out_shape=jax.ShapeDtypeStruct((3 * N, B), f32),
        in_specs=[vm],
        out_specs=vm,
        scratch_shapes=[V((N, N), f32), V((B, B), f32), V((N, 2 * B), bf16), V((2 * B, N), bf16), V((B, N), bf16)],
        compiler_params=pltpu.CompilerParams(vmem_limit_bytes=24 * 1024 * 1024),
        cost_estimate=pl.CostEstimate(flops=17_000_000_000, bytes_accessed=2_000_000, transcendentals=0),
        name="first_blocks",
    )(a0)


def panel_solve(ids, gathered, factors):
    W = gathered.shape[1]
    RR = W - PR
    n_col = PR // (PANELS * BS)

    def kern(id_ref, pr_ref, f0, vth, vtl, xc, E, D, Y, G, LBT, YQ, GQ, LQ, LT, RHH, RLO, ZPH, ZPL, LRH, LRL, PV, XT, sems):
        copies = []
        for p in range(PANELS):
            for c in range(n_col):
                n = c * PANELS + p
                copies.append(
                    pltpu.make_async_copy(
                        pr_ref.at[pl.ds(n * BS, BS), :], E.at[pl.ds(p * NB + c * BS, BS), :], sems.at[n]
                    )
                )
        for copy in copies:
            copy.start()
        for copy in copies[: B // BS]:
            copy.wait()
        rid = id_ref[0]
        cid = id_ref[1]
        second = rid >= NB // BS
        lane_r = lax.broadcasted_iota(jnp.int32, (B, RR), 1)

        def panel_chunks(q, q0, first):
            def yq():
                return YQ[0], YQ[1]

            def gq():
                return GQ[0], GQ[1]

            def keep(c0, w, h, l):
                RHH[0:B, c0 : c0 + w] = h
                RHH[B : 2 * B, c0 : c0 + w] = h
                RLO[:, c0 : c0 + w] = l

            def row_panel(c0, w):
                def f():
                    h, l = split(dot3(yq(), split(E[pl.ds(q0, B), c0 : c0 + w]), NN))
                    keep(c0, w, h, l)
                    ZPH[pl.ds(q0, B), c0 : c0 + w] = h
                    ZPL[pl.ds(q0, B), c0 : c0 + w] = l

                return f

            def pivot_columns():
                h, l = yq()
                RHH[0:B, pl.ds(q0, B)] = h
                RHH[B : 2 * B, pl.ds(q0, B)] = h
                RLO[:, pl.ds(q0, B)] = l
                ZPH[pl.ds(q0, B), pl.ds(q0, B)] = h
                ZPL[pl.ds(q0, B), pl.ds(q0, B)] = l
                E[first * B : PR, pl.ds(q0, B)] = jnp.zeros((PR - first * B, B), f32)

            def r_panel():
                e = split(E[pl.ds(q0, B), PR:W])
                zp = split(dot3(yq(), e, NN))
                keep(PR, RR, *zp)
                XT[pl.ds(q0, B), :] = dot3((LQ[0], LQ[1]), zp, NN)
                z = dot3(gq(), e, NN)
                live = jnp.logical_and(second, q < NB // B)
                z = jnp.where(jnp.logical_and(lane_r < BS, jnp.logical_not(live)), 0.0, z)
                h, l = split(z.T)
                LRH[:, pl.ds(q0, B)] = h
                LRL[:, pl.ds(q0, B)] = l

            def last_pivot():
                ZPH[pl.ds(q0, B), pl.ds(q0, B)] = YQ[0]
                ZPL[pl.ds(q0, B), pl.ds(q0, B)] = YQ[1]

            def col_panel(j):
                def f():
                    h, l = split(dot3(split(E[j * B : (j + 1) * B, pl.ds(q0, B)]), gq(), NT))
                    LT[j * B : (j + 1) * B, 0:B] = h
                    LT[j * B : (j + 1) * B, B : 2 * B] = l

                return f

            chunks = []
            chunks += [col_panel(j) for j in range(first, KB)]
            chunks += [row_panel(c0, 256) for c0 in range(0, PR, 256)]
            return chunks + [pivot_columns, r_panel] if first < KB else chunks + [last_pivot, r_panel]

        def trail_chunks(first):
            def trail(j, c0, w):
                def f():
                    rows = slice(j * B, (j + 1) * B)
                    u = dot(LT[rows, :], RHH[:, c0 : c0 + w], NN)
                    u = u + dot(LT[rows, 0:B], RLO[:, c0 : c0 + w], NN)
                    E[rows, c0 : c0 + w] = E[rows, c0 : c0 + w] - u

                return f

            parts = [(c0, 512) for c0 in range(0, PR, 512)] + [(PR, RR)]
            return [trail(j, c0, w) for j in range(first, KB) for c0, w in parts]

        for k in range(KA):
            for n, ref in enumerate((YQ, GQ, LQ)):
                ref[0], ref[1] = split(f0[(n * KA + k) * B : (n * KA + k + 1) * B, :])
            if k == 0:
                chunks = panel_chunks(k, k * B, k + 1)
                drain(chunks[KB - 1 : KB + 3])
                for copy in copies[B // BS :]:
                    copy.wait()
                drain(chunks[: KB - 1] + chunks[KB + 3 :] + trail_chunks(k + 1))
            elif k < KA - 1:
                drain(panel_chunks(k, k * B, k + 1) + trail_chunks(k + 1))
        crit(E, D, (YQ[0], YQ[1]), (GQ[0], GQ[1]), (KA - 1) * B, KA * B)

        def factor(chunks):
            n = len(chunks)

            def fill(s):
                drain(chunks[n * s // 16 : n * (s + 1) // 16])

            factor128(D, Y, G, LBT, fill)
            for q_ref, ref in ((YQ, Y), (GQ, G), (LQ, LBT)):
                q_ref[0], q_ref[1] = split(ref[...])

        def body(k, carry):
            q0 = pl.multiple_of((k - 1) * B, B)
            k0 = pl.multiple_of(k * B, B)
            n0 = pl.multiple_of((k + 1) * B, B)
            factor(panel_chunks(k - 1, q0, KA) + trail_chunks(KA))
            crit(E, D, split(Y[...]), split(G[...]), k0, n0)
            return carry

        def inverse(rows, c0):
            z = (ZPH[rows, c0 : c0 + 256], ZPL[rows, c0 : c0 + 256])
            return dot3((LRH[:, rows], LRL[:, rows]), z, NN)

        def partial(c0):
            def f():
                for ref in (ZPH, ZPL):
                    ref[c0 : c0 + B, c0 + B : c0 + 2 * B] = jnp.zeros((B, B), bf16)
                PV[:, c0 : c0 + 256] = inverse(slice(c0, last), c0)

            return f

        lax.fori_loop(KA, KB - 1, body, 0)
        last = (KB - 1) * B
        steps = range(0, PR, 256)
        factor(panel_chunks(KB - 2, last - B, KB - 1) + trail_chunks(KB - 1) + [partial(c0) for c0 in steps])
        drain(panel_chunks(KB - 1, last, KB))
        for c0 in steps:
            h, l = split(PV[:, c0 : c0 + 256] + inverse(slice(last, PR), c0))
            vth[:, c0 : c0 + 256] = h
            vtl[:, c0 : c0 + 256] = l
        for p in range(PANELS):
            c0 = pl.multiple_of(cid * BS + p * NB, BS)
            x = XT[pl.ds(c0, BS), :]
            col = c0 + lax.broadcasted_iota(jnp.int32, (BS, RR), 0)
            ln = lax.broadcasted_iota(jnp.int32, (BS, RR), 1)
            x = jnp.where(jnp.logical_and(ln < BS, col > rid * BS + ln), 0.0, x)
            xc[:, BS * p : BS * (p + 1)] = x.T

    vm = pl.BlockSpec(memory_space=pltpu.VMEM)
    V = pltpu.VMEM
    out = jax.ShapeDtypeStruct((RR, PR), bf16)
    return pl.pallas_call(
        kern,
        out_shape=(out, out, jax.ShapeDtypeStruct((RR, PANELS * BS), f32)),
        in_specs=[pl.BlockSpec(memory_space=pltpu.SMEM), pl.BlockSpec(memory_space=pl.ANY), vm],
        out_specs=(vm, vm, vm),
        scratch_shapes=[
            V((PR, W), f32),
            V((B, B), f32),
            V((B, B), f32),
            V((B, B), f32),
            V((B, B), f32),
            V((2, B, B), bf16),
            V((2, B, B), bf16),
            V((2, B, B), bf16),
            V((PR, 2 * B), bf16),
            V((2 * B, W), bf16),
            V((B, W), bf16),
            V((PR, PR), bf16),
            V((PR, PR), bf16),
            V((RR, PR), bf16),
            V((RR, PR), bf16),
            V((RR, PR), f32),
            V((PR, RR), f32),
            pltpu.SemaphoreType.DMA((PANELS * n_col,)),
        ],
        compiler_params=pltpu.CompilerParams(vmem_limit_bytes=58 * 1024 * 1024),
        cost_estimate=pl.CostEstimate(flops=46_000_000_000, bytes_accessed=8_000_000, transcendentals=0),
        name="panel_solve",
    )(ids, gathered, factors)


def trailing_update(vth, vtl, xc, a_cols, local):
    RR, CC = local.shape
    step = 256

    def kern(vth, vtl, xc, ac, al, out):
        out[...] = al[...] - dot3((vth[...], vtl[...]), split(ac[...]), NN)

        @pl.when(pl.program_id(0) == 0)
        def _():
            out[:, 0 : PANELS * BS] = xc[...]

    whole = lambda a: pl.BlockSpec(a.shape, lambda i: (0, 0))
    part = lambda rows: pl.BlockSpec((rows, step), lambda i: (0, i))
    return pl.pallas_call(
        kern,
        grid=(CC // step,),
        out_shape=jax.ShapeDtypeStruct((RR, CC), f32),
        in_specs=[whole(vth), whole(vtl), whole(xc), part(PR), part(RR)],
        out_specs=part(RR),
        compiler_params=pltpu.CompilerParams(vmem_limit_bytes=62 * 1024 * 1024),
        name="trailing_update",
    )(vth, vtl, xc, a_cols, local)


def shards(matrix):
    rid = lax.axis_index(("y", "x"))
    cid = lax.axis_index(("z", "k"))
    ids = jnp.stack([rid, cid]).astype(jnp.int32)
    n_row = lax.axis_size(("y", "x"))
    thin = PANELS * BS
    block = matrix[:BS, :thin].reshape(1, BS * thin // 128, 128)
    block = jnp.broadcast_to(block, (n_row, BS * thin // 128, 128))
    own = lax.all_to_all(block, ("y", "x"), 0, 0, tiled=True).reshape(PR, thin).T
    mine = jnp.concatenate([own, matrix[:, :thin].T], axis=1)
    early = own[:BS, : KA * B]
    mine, early, top = lax.optimization_barrier((mine, early, matrix[:BS]))
    top = jnp.broadcast_to(top[None], (n_row,) + top.shape)
    a_cols = lax.all_to_all(top, ("y", "x"), 0, 0, tiled=True).reshape(PR, top.shape[2])
    gathered = lax.all_gather(mine, ("z", "k"), axis=0, tiled=True)
    early = lax.all_gather(early, ("z", "k"), axis=0, tiled=True)
    factors = first_blocks(early)
    vth, vtl, xc = panel_solve(ids, gathered, factors)
    return trailing_update(vth, vtl, xc, a_cols, matrix)


def solution(mesh):
    four = Mesh(mesh.devices.reshape(8, 4, 8, 2), ("y", "x", "z", "k"))
    placed = P(("y", "x"), ("z", "k"))
    return jax.shard_map(shards, mesh=four, in_specs=(placed,), out_specs=placed, check_vma=False)
```
